128 devices in a mesh: node: 8 (over z, core), local: 16 (over x, y).
Axes of the slice: x: 4, y: 4, z: 4, core: 2. Of those that a mesh axis runs over, the one named last changes fastest.
Arguments:
- tokens: bfloat16 [2, 1024, 7168], P(None, ('node', 'local')), may hold values from -6 to 6
- routes: int32 [2, 1024, 8], P(None, ('node', 'local')), may hold values from 0 to 63, as said below
- route_weight: float32 [2, 1024, 8], P(None, ('node', 'local')), may hold values from 0.1 to 1
- gate_weight: bfloat16 [128, 7168, 512], P(('node', 'local')), may hold values from -0.0625 to 0.0625
- up_weight: bfloat16 [128, 7168, 512], P(('node', 'local')), may hold values from -0.0625 to 0.0625
- down_weight: bfloat16 [128, 512, 7168], P(('node', 'local')), may hold values from -0.1875 to 0.1875
Outputs:
- mixed: bfloat16 [2, 1024, 7168], P(None, ('node', 'local'))
The draws below stay inside these ranges and needn't reach their ends.
Inputs may be any that keep to these rules, and one draw needn't show every extreme that they name: `routes`: node group g holds the experts e with e // 8 = g. Each token's choices lie in exactly 4 node groups, 2 in each, and no token chooses an expert twice. Among the 8 rows of one device in one micro-batch, no expert is chosen more than 2 times, and no node group is chosen by more than 8 tokens.
All inputs are finite; a program needn't handle non-finite values.
Results may differ from the reference program's by a relative error of at most 0.0058.
Values may be sent and summed in bfloat16 or wider, within the bound.
No kernel may reach another device: no remote copies, remote signals or barrier semaphores. Data moves between devices by JAX's collectives and lax.ppermute only.
A program may use at most 128 MiB of HBM per device.

```python
import math
import jax
import jax.numpy as jnp
from jax import lax

D = 7168
FF = 1024
TOPK = 8
NODE_LIMIT = 4
MICRO = 2
TOK_DEV = 8
EXPERTS = 64
GROUP_EXPERTS = 8
PICKS = 2
SLOT = 2
TOKENS = 1024
N_NODE = 8


def draw_routes(key, part):
    key = jax.random.fold_in(key, 11)
    blocks = MICRO * TOKENS // TOK_DEV
    key_hot, key_node, key_perm = jax.random.split(key, 3)
    node_ids = jnp.arange(N_NODE, dtype=jnp.int32)
    hot = jax.random.randint(key_hot, (blocks,), 0, N_NODE)
    scores = jax.random.randint(key_node, (blocks, TOK_DEV, N_NODE), 0, 1 << 20) * N_NODE + node_ids[None, None, :]
    scores = jnp.where(node_ids[None, None, :] == hot[:, None, None], 1 << 30, scores)
    chosen = lax.top_k(scores, NODE_LIMIT)[1].astype(jnp.int32)
    member = jnp.max((chosen[:, :, :, None] == node_ids[None, None, None, :]).astype(jnp.int32), 2)
    before = jnp.cumsum(member, 1) - member
    order = jnp.take_along_axis(before, chosen, axis=2)
    index = (PICKS * order[:, :, :, None] + jnp.arange(PICKS, dtype=jnp.int32)[None, None, None, :]) % GROUP_EXPERTS
    perm_scores = jax.random.randint(key_perm, (blocks, N_NODE, GROUP_EXPERTS), 0, 1 << 20) * GROUP_EXPERTS + jnp.arange(GROUP_EXPERTS, dtype=jnp.int32)[None, None, :]
    perm = jnp.argsort(perm_scores, axis=2).astype(jnp.int32)
    block_ids = jnp.arange(blocks, dtype=jnp.int32)[:, None, None, None]
    within = perm[block_ids, chosen[:, :, :, None], index]
    experts = chosen[:, :, :, None] * GROUP_EXPERTS + within
    return experts.reshape(MICRO, TOKENS, TOPK).astype(jnp.int32)


def block_scale(rng, shape, shards, least, high):
    loudness, own = 1.0, jax.random.fold_in(rng, 6)
    for dim, shards_of in shards:
        draws = jnp.exp(jax.random.uniform(jax.random.fold_in(own, dim), (shards_of,), jnp.float32, least / len(shards), high / len(shards)))
        loudness = loudness * jnp.repeat(draws, shape[dim] // shards_of).reshape([-1 if axis == dim else 1 for axis in range(len(shape))])
    return loudness


def scatter_about(key, shape, scale, reach, pieces=(), kind=jnp.bfloat16):
    gain = block_scale(key, shape, pieces, -0.22, 0.18) if pieces else 1.0
    values = jax.random.normal(key, shape, jnp.float32) * scale * gain
    return jnp.minimum(jnp.maximum(values, -reach), reach).astype(kind)


def setup_inputs(seed: int = 0) -> dict:
    splits = jax.random.split(jax.random.key(seed), 7)
    return {
        "tokens": scatter_about(splits[0], (MICRO, TOKENS, D), 1.0, 6.0, ((1, 128),)),
        "routes": draw_routes(jax.random.fold_in(splits[6], 71), 0),
        "route_weight": jnp.clip(jnp.exp(math.log(1.0) - 2.3025851 * jax.random.uniform(splits[2], (MICRO, TOKENS, TOPK), jnp.float32) ** block_scale(splits[2], (MICRO, TOKENS, TOPK), ((1, 128),), -0.2, 0.2)), 0.1, 1.0),
        "gate_weight": scatter_about(splits[3], (2 * EXPERTS, D, FF // 2), D ** -0.5, 0.0625, ((0, 128),)),
        "up_weight": scatter_about(splits[4], (2 * EXPERTS, D, FF // 2), D ** -0.5, 0.0625, ((0, 128),)),
        "down_weight": scatter_about(splits[5], (2 * EXPERTS, FF // 2, D), FF ** -0.5, 0.1875, ((0, 128),)),
    }


def expert_rows(rows, gate_pair, up_pair, down_pair):
    gate_act = jnp.dot(rows, gate_pair, preferred_element_type=jnp.float32)
    up_act = jnp.dot(rows, up_pair, preferred_element_type=jnp.float32)
    hidden = (jax.nn.silu(gate_act) * up_act).astype(jnp.bfloat16)
    return jnp.dot(hidden, down_pair, preferred_element_type=jnp.float32).astype(jnp.bfloat16)


def reference(tokens, routes, route_weight, gate_weight, up_weight, down_weight):
    blocks = TOKENS // TOK_DEV
    assign = TOK_DEV * TOPK
    half_width = FF // 2
    gate_all = gate_weight.reshape(EXPERTS, 2, D, half_width)
    up_all = up_weight.reshape(EXPERTS, 2, D, half_width)
    down_all = down_weight.reshape(EXPERTS, 2, half_width, D)
    results = []
    for batch in range(MICRO):
        route_row = routes[batch].reshape(blocks, assign)
        onehot = (route_row[:, :, None] == jnp.arange(EXPERTS, dtype=jnp.int32)[None, None, :]).astype(jnp.int32)
        slot_rank = jnp.sum((jnp.cumsum(onehot, 1) - onehot) * onehot, 2)
        position = (route_row * (blocks * SLOT) + jnp.arange(blocks, dtype=jnp.int32)[:, None] * SLOT + slot_rank).reshape(-1).astype(jnp.int32)
        token_ids = jnp.repeat(jnp.arange(TOKENS, dtype=jnp.int32), TOPK)
        table = jnp.full((EXPERTS * blocks * SLOT,), TOKENS, jnp.int32).at[position].set(token_ids)
        table = table.reshape(EXPERTS, blocks * SLOT)
        padded = jnp.concatenate([tokens[batch], jnp.zeros((1, D), tokens.dtype)], 0)

        def one_expert(expert_id):
            rows = padded[table[expert_id]]
            gate_pair = jnp.concatenate([gate_all[expert_id, 0], gate_all[expert_id, 1]], 1)
            up_pair = jnp.concatenate([up_all[expert_id, 0], up_all[expert_id, 1]], 1)
            down_pair = jnp.concatenate([down_all[expert_id, 0], down_all[expert_id, 1]], 0)
            return expert_rows(rows, gate_pair, up_pair, down_pair)

        outputs = lax.map(one_expert, jnp.arange(EXPERTS, dtype=jnp.int32))
        picked = outputs.reshape(-1, D)[position].reshape(TOKENS, TOPK, D).astype(jnp.float32)
        mixed = jnp.einsum("tk,tkd->td", route_weight[batch].astype(jnp.float32), picked, precision=lax.Precision.HIGHEST)
        results.append(mixed.astype(jnp.bfloat16))
    return jnp.stack(results, 0)
```

```python
import functools

import jax
import jax.numpy as jnp
from jax import lax
from jax.experimental import pallas as pl
from jax.experimental.pallas import tpu as pltpu
from jax.sharding import PartitionSpec as P

AXES = ("node", "local")
ORDERS = (("x", "y", "z"), ("y", "z", "x"), ("z", "x", "y"))
RING = 4
META = 128
PARAMS = pltpu.CompilerParams(vmem_limit_bytes=48 * 1024 * 1024)
BF16, F32 = jnp.bfloat16, jnp.float32


def device_index(place):
    return (place["z"] * 2 + place["c"]) * 16 + place["x"] * 4 + place["y"]


def all_places():
    return [
        {"z": z, "c": c, "x": x, "y": y}
        for z in range(4)
        for c in range(2)
        for x in range(4)
        for y in range(4)
    ]


def from_offset(value, axis, offset):
    size = 2 if axis == "c" else RING
    pairs = []
    for place in all_places():
        target = dict(place)
        target[axis] = (place[axis] - offset) % size
        pairs.append((device_index(place), device_index(target)))
    return lax.ppermute(value, AXES, pairs)


def column_split(width):
    tiles = width // 128
    sizes = [(tiles + 2 - k) // 3 * 128 for k in range(3)]
    starts = [sum(sizes[:k]) for k in range(3)]
    return starts, sizes


def cost(flops, nbytes):
    return pl.CostEstimate(flops=int(flops), bytes_accessed=int(nbytes), transcendentals=0)


def iota(shape, dim):
    return lax.broadcasted_iota(jnp.int32, shape, dim)


def prep_kernel(starts, sizes, tok_ref, info_ref, *outs):
    info = info_ref[...]
    lane = iota(info.shape, 1)
    high = info.astype(BF16)
    low = (info - high.astype(F32)).astype(BF16)
    meta = jnp.where(lane < 16, high.astype(F32), low.astype(F32)).astype(BF16)
    for out, start, size in zip(outs, starts, sizes, strict=True):
        out[:, :size] = tok_ref[:, start : start + size]
        out[:, size:] = meta


def prepare(tokens, info, starts, sizes):
    rows = tokens.shape[0]
    return pl.pallas_call(
        functools.partial(prep_kernel, starts, sizes),
        out_shape=[jax.ShapeDtypeStruct((rows, size + META), BF16) for size in sizes],
        compiler_params=PARAMS,
        cost_estimate=cost(0, 4 * tokens.size),
        name="prep",
    )(tokens, info)


def slot_matrix(meta, experts, weighted):
    meta = meta.astype(F32)
    shape = meta.shape
    row, lane = iota(shape, 0), iota(shape, 1)
    chosen = jnp.zeros(shape, F32)
    weight = jnp.zeros(shape, F32)
    if weighted:
        gains = pltpu.roll(meta, META - 8, 1) + pltpu.roll(meta, META - 16, 1)
    for o3 in range(RING):
        hit = (meta == experts[o3].astype(F32)) & (lane < 8)
        here = lane // 16 == o3
        match = jnp.max(jnp.where(hit, 1.0, 0.0), axis=1, keepdims=True)
        chosen = jnp.where(here, match, chosen)
        if weighted:
            gain = jnp.sum(jnp.where(hit, gains, 0.0), axis=1, keepdims=True)
            weight = jnp.where(here, gain, weight)
    near = (shape[0], shape[0])
    before = (iota(near, 0) // 8 == iota(near, 1) // 8) & (iota(near, 1) < iota(near, 0))
    rank = jnp.dot(
        jnp.where(before, 1.0, 0.0).astype(BF16), chosen.astype(BF16), preferred_element_type=F32
    )
    keep = (rank == (lane % 2).astype(F32)) & (row // 8 == lane % 16 // 2)
    return jnp.where(keep, chosen * weight if weighted else chosen, 0.0)


def pack_kernel(size, color, experts_ref, *refs):
    blocks, outs = refs[:8], refs[8:]
    experts = [experts_ref[color, o3] for o3 in range(RING)]
    for j, block in enumerate(blocks):
        matrix = slot_matrix(block[:, size:], experts, False).astype(BF16)
        packed = lax.dot_general(
            matrix[:, :64],
            block[:, :size],
            (((0,), (0,)), ((), ())),
            preferred_element_type=F32,
        ).astype(BF16)
        for o3 in range(RING):
            outs[o3][16 * j : 16 * j + 16, :] = packed[16 * o3 : 16 * o3 + 16]


def pack(blocks, experts, color, size):
    return pl.pallas_call(
        functools.partial(pack_kernel, size, color),
        out_shape=[jax.ShapeDtypeStruct((128, size), BF16)] * RING,
        in_specs=[pl.BlockSpec(memory_space=pltpu.SMEM)]
        + [pl.BlockSpec(memory_space=pltpu.VMEM)] * 8,
        compiler_params=PARAMS,
        cost_estimate=cost(2 * 64 * 512 * size, 2 * 1024 * size),
        name=f"pack{color}",
    )(experts, *blocks)


def chunk_order(color):
    sizes = {"x": 4, "y": 4, "z": 4, "c": 2}

    def dims(k):
        a1, a2, a3 = ORDERS[k]
        return (a3, "c", a2, a1)

    order = []
    for i in range(128):
        place, rest = {}, i
        for axis in reversed(dims(0)):
            place[axis], rest = rest % sizes[axis], rest // sizes[axis]
        j = 0
        for axis in dims(color):
            j = j * sizes[axis] + place[axis]
        order.append(j)
    return order


def project_kernel(color, start, size, last, *refs):
    refs = list(refs)
    rows = [refs.pop(0) for _ in range(RING)]
    gate_ref, up_ref = refs.pop(0), refs.pop(0)
    before = refs.pop(0) if color else None
    outs = [refs.pop(0) for _ in range(3 if last else 1)]
    held, gate, up, part, sems = refs
    width = gate.shape[1]
    loads = [
        pltpu.make_async_copy(rows[o3], held.at[pl.ds(128 * o3, 128)], sems.at[o3])
        for o3 in range(RING)
    ]
    loads.append(pltpu.make_async_copy(gate_ref.at[pl.ds(start, size)], gate, sems.at[4]))
    loads.append(pltpu.make_async_copy(up_ref.at[pl.ds(start, size)], up, sems.at[5]))
    for load in loads:
        load.start()
    for load in loads[:5]:
        load.wait()
    acc = part if color else outs[0]
    for half, weight in enumerate((gate, up)):
        if half:
            loads[5].wait()

        @pl.loop(0, width // 256)
        def _(n, weight=weight, half=half):
            at = pl.multiple_of(n * 256, 256)
            to = pl.multiple_of(half * width + n * 256, 256)
            acc[:, pl.ds(to, 256)] = jnp.dot(
                held[...], weight[:, pl.ds(at, 256)], preferred_element_type=F32
            )

    if not color:
        return
    order = chunk_order(color)
    for i in range(0, 128, 2):
        mine = jnp.concatenate([part[4 * j : 4 * j + 4, :] for j in order[i : i + 2]], axis=0)
        total = before[4 * i : 4 * i + 8, :] + mine
        if not last:
            outs[0][4 * i : 4 * i + 8, :] = total
        else:
            gated, upped = total[:, :width], total[:, width:]
            before[4 * i : 4 * i + 8, :width] = gated / (1.0 + jnp.exp(-gated)) * upped
    if last:
        for k, out in enumerate(outs):
            to_own = chunk_order(k)
            from_own = [to_own.index(j) for j in range(128)]
            for j in range(0, 128, 4):
                out[4 * j : 4 * j + 16, :] = jnp.concatenate(
                    [before[4 * i : 4 * i + 4, :width] for i in from_own[j : j + 4]], axis=0
                ).astype(BF16)


def project(rows, gate, up, before, color, start, size, last):
    width = gate.shape[1]
    everywhere = pl.BlockSpec(memory_space=pl.ANY)
    in_vmem = pl.BlockSpec(memory_space=pltpu.VMEM)
    operands = [*rows, gate, up]
    if color:
        operands.append(before)
    if last:
        outs = [jax.ShapeDtypeStruct((512, width), BF16)] * 3
    else:
        outs = [jax.ShapeDtypeStruct((512, 2 * width), F32)]
    return pl.pallas_call(
        functools.partial(project_kernel, color, start, size, last),
        out_shape=outs,
        in_specs=[everywhere] * 6 + [in_vmem] * (len(operands) - 6),
        scratch_shapes=[
            pltpu.VMEM((512, size), BF16),
            pltpu.VMEM((size, width), BF16),
            pltpu.VMEM((size, width), BF16),
            pltpu.VMEM((512, 2 * width) if color else (8, 128), F32),
            pltpu.SemaphoreType.DMA((6,)),
        ],
        compiler_params=PARAMS,
        cost_estimate=cost(4 * 512 * size * width, 4 * size * width + 2 * 512 * size),
        name=f"project{color}",
    )(*operands)


def down_kernel(start, size, hidden_ref, down_ref, *refs):
    outs, held, sem = refs[:RING], refs[RING], refs[RING + 1]
    load = pltpu.make_async_copy(down_ref.at[:, pl.ds(start, size)], held, sem)
    load.start()
    load.wait()
    for n in range(0, size, 256):
        step = min(256, size - n)
        value = jnp.dot(
            hidden_ref[...], held[:, n : n + step], preferred_element_type=F32
        ).astype(BF16)
        for o3 in range(RING):
            outs[o3][:, n : n + step] = value[128 * o3 : 128 * o3 + 128]


def project_down(hidden, down, color, start, size):
    return pl.pallas_call(
        functools.partial(down_kernel, start, size),
        out_shape=[jax.ShapeDtypeStruct((128, size), BF16)] * RING,
        in_specs=[pl.BlockSpec(memory_space=pltpu.VMEM), pl.BlockSpec(memory_space=pl.ANY)],
        scratch_shapes=[pltpu.VMEM((down.shape[0], size), BF16), pltpu.SemaphoreType.DMA(())],
        compiler_params=PARAMS,
        cost_estimate=cost(2 * 512 * size * 512, 4 * 512 * size),
        name=f"down{color}",
    )(hidden, down)


def weighted_block(meta_ref, back, experts, j):
    matrix = slot_matrix(meta_ref[...], experts, True)[:, :64]
    high = matrix.astype(BF16)
    low = (matrix - high.astype(F32)).astype(BF16)
    rows = jnp.concatenate([ref[16 * j : 16 * j + 16, :] for ref in back], axis=0)
    return jnp.dot(high, rows, preferred_element_type=F32) + jnp.dot(
        low, rows, preferred_element_type=F32
    )


def other_kernel(color, experts_ref, *refs):
    metas, back, outs = refs[:4], refs[4:8], refs[8:]
    experts = [experts_ref[color, o3] for o3 in range(RING)]
    for o2 in range(RING):
        outs[o2][...] = weighted_block(metas[o2], back, experts, 4 + o2).astype(BF16)


def own_kernel(color, experts_ref, *refs):
    metas, back, swapped, outs = refs[:4], refs[4:8], refs[8:12], refs[12:]
    experts = [experts_ref[color, o3] for o3 in range(RING)]
    for o2 in range(RING):
        total = weighted_block(metas[o2], back, experts, o2) + swapped[o2][...].astype(F32)
        outs[o2][...] = total.astype(outs[o2].dtype)


def combine(blocks, back, swapped, experts, color, size):
    own = swapped is not None
    in_vmem = pl.BlockSpec(memory_space=pltpu.VMEM)
    meta_spec = pl.BlockSpec((64, META), lambda i: (0, size // META))
    whole = lambda rows: pl.BlockSpec((rows, size), lambda i: (0, 0))
    operands = [experts, *blocks, *back, *(swapped or [])]
    specs = [pl.BlockSpec(memory_space=pltpu.SMEM)] + [meta_spec] * 4 + [whole(128)] * 4
    specs += [whole(64)] * 4 if own else []
    kinds = [F32 if own and o2 == 0 else BF16 for o2 in range(RING)]
    return pl.pallas_call(
        functools.partial(own_kernel if own else other_kernel, color),
        grid=(1,),
        out_shape=[jax.ShapeDtypeStruct((64, size), kind) for kind in kinds],
        in_specs=specs,
        out_specs=[whole(64)] * 4,
        compiler_params=PARAMS,
        cost_estimate=cost(4 * 256 * 64 * size, 2 * 512 * size),
        name=f"{'own' if own else 'other'}{color}",
    )(*operands)


def sum_kernel(mine_ref, *refs):
    arrived, outs = refs[:3], refs[3:]
    total = mine_ref[...]
    for ref in arrived:
        total = total + ref[...].astype(F32)
    for o1, out in enumerate(outs):
        out[...] = total[16 * o1 : 16 * o1 + 16].astype(out.dtype)


def sum_blocks(mine, arrived, color, size):
    kinds = [F32, BF16, BF16, BF16]
    return pl.pallas_call(
        sum_kernel,
        out_shape=[jax.ShapeDtypeStruct((16, size), kind) for kind in kinds],
        compiler_params=PARAMS,
        cost_estimate=cost(256 * size, 1024 * size),
        name=f"sum{color}",
    )(mine, *arrived)


def finish_kernel(starts, sizes, *refs):
    out = refs[-1]
    for k, (start, size) in enumerate(zip(starts, sizes, strict=True)):
        total = refs[4 * k][...]
        for ref in refs[4 * k + 1 : 4 * k + 4]:
            total = total + ref[...].astype(F32)
        out[:, start : start + size] = total.astype(BF16)


def finish(pieces, starts, sizes, rows, width):
    return pl.pallas_call(
        functools.partial(finish_kernel, starts, sizes),
        out_shape=jax.ShapeDtypeStruct((rows, width), BF16),
        compiler_params=PARAMS,
        cost_estimate=cost(4 * rows * width, 10 * rows * width),
        name="finish",
    )(*pieces)


def body(tokens, routes, route_weight, gate_weight, up_weight, down_weight):
    micro, count, width = tokens.shape
    rows = micro * count
    choices = routes.shape[2]
    starts, sizes = column_split(width)
    node, local = lax.axis_index("node"), lax.axis_index("local")
    here = {"z": node // 2, "c": node % 2, "x": local // 4, "y": local % 4}

    def expert_at(axis, offset):
        place = dict(here)
        place[axis] = (here[axis] - offset) % RING
        return (place["z"] * 2 + place["c"]) * 8 + (place["x"] * 4 + place["y"]) // 2

    experts = jnp.stack(
        [jnp.stack([expert_at(order[2], o3) for o3 in range(RING)]) for order in ORDERS]
    ).astype(jnp.int32)
    gains = route_weight.reshape(rows, choices)
    info = jnp.concatenate(
        [
            routes.reshape(rows, choices).astype(F32),
            gains,
            gains,
            jnp.zeros((rows, META - 3 * choices), F32),
        ],
        axis=1,
    )
    own_rows = prepare(tokens.reshape(rows, width), info, starts, sizes)

    blocks, arrived = [], []
    first = [
        [own_rows[k]] + [from_offset(own_rows[k], ORDERS[k][0], o) for o in (1, 3, 2)]
        for k in range(3)
    ]
    for k in range(3):
        a1, a2, a3 = ORDERS[k]
        by_offset = dict(zip((0, 1, 3, 2), first[k], strict=True))
        block = jnp.concatenate([by_offset[o] for o in range(RING)], axis=0)
        own = {0: block}
        for o in (1, 3, 2):
            own[o] = from_offset(block, a2, o)
        own = [own[o] for o in range(RING)]
        other = [from_offset(value, "c", 1) for value in own]
        blocks.append((own, other))
    for k in range(3):
        own, other = blocks[k]
        packed = pack(own + other, experts, k, sizes[k])
        got = {0: packed[0]}
        for o in (1, 3, 2):
            got[o] = from_offset(packed[o], ORDERS[k][2], o)
        arrived.append([got[o] for o in range(RING)])

    total = None
    for k in range(3):
        total = project(
            arrived[k], gate_weight[0], up_weight[0], total, k, starts[k], sizes[k], k == 2
        )
        if k < 2:
            total = total[0]
    hidden = total

    pieces = []
    for k in range(3):
        a1, a2, a3 = ORDERS[k]
        outs = project_down(hidden[k], down_weight[0], k, starts[k], sizes[k])
        got = {0: outs[0]}
        for o in (1, 3, 2):
            got[o] = from_offset(outs[o], a3, -o)
        back = [got[o] for o in range(RING)]
        own, other = blocks[k]
        theirs = combine(other, back, None, experts, k, sizes[k])
        swapped = [from_offset(value, "c", 1) for value in theirs]
        sums = combine(own, back, swapped, experts, k, sizes[k])
        moved = [from_offset(sums[o], a2, -o) for o in (1, 3, 2)]
        parts = sum_blocks(sums[0], moved, k, sizes[k])
        pieces.append(parts[0])
        pieces += [from_offset(parts[o], a1, -o) for o in (1, 3, 2)]
    return finish(pieces, starts, sizes, rows, width).reshape(micro, count, width)


def solution(mesh):
    placed = (
        P(None, AXES, None),
        P(None, AXES, None),
        P(None, AXES, None),
        P(AXES, None, None),
        P(AXES, None, None),
        P(AXES, None, None),
    )
    return jax.shard_map(
        body,
        mesh=mesh,
        in_specs=placed,
        out_specs=P(None, AXES, None),
        check_vma=False,
    )
```

```python
import functools

import jax
import jax.numpy as jnp
from jax import lax
from jax.experimental import pallas as pl
from jax.experimental.pallas import tpu as pltpu
from jax.sharding import PartitionSpec as P

AXES = ("node", "local")
ORDERS = (("x", "y", "z"), ("y", "z", "x"), ("z", "x", "y"))
RING = 4
META = 128
PARAMS = pltpu.CompilerParams(vmem_limit_bytes=24 * 1024 * 1024)
BF16, F32 = jnp.bfloat16, jnp.float32


def device_index(place):
    return (place["z"] * 2 + place["c"]) * 16 + place["x"] * 4 + place["y"]


def all_places():
    return [
        {"z": z, "c": c, "x": x, "y": y}
        for z in range(4)
        for c in range(2)
        for x in range(4)
        for y in range(4)
    ]


def from_offset(value, axis, offset):
    size = 2 if axis == "c" else RING
    pairs = []
    for place in all_places():
        sign = -1 if place["c"] else 1
        target = dict(place)
        target[axis] = (place[axis] - sign * offset) % size
        pairs.append((device_index(place), device_index(target)))
    return lax.ppermute(value, AXES, pairs)


def column_split(width):
    tiles = width // 128
    sizes = [(tiles + 2 - k) // 3 * 128 for k in range(3)]
    starts = [sum(sizes[:k]) for k in range(3)]
    return starts, sizes


def cost(flops, nbytes):
    return pl.CostEstimate(flops=int(flops), bytes_accessed=int(nbytes), transcendentals=0)


def iota(shape, dim):
    return lax.broadcasted_iota(jnp.int32, shape, dim)


def prep_kernel(starts, sizes, tok_ref, info_ref, tok2_ref, info2_ref, *outs):
    half = tok_ref.shape[0]
    for part, (tok, info_in) in enumerate(((tok_ref, info_ref), (tok2_ref, info2_ref))):
        info = info_in[...]
        lane = iota(info.shape, 1)
        high = info.astype(BF16)
        low = (info - high.astype(F32)).astype(BF16)
        meta = jnp.where(lane < 16, high.astype(F32), low.astype(F32)).astype(BF16)
        at = slice(part * half, part * half + half)
        for k, (start, size) in enumerate(zip(starts, sizes, strict=True)):
            outs[k][at, :size] = tok[:, start : start + size]
            outs[k][at, size:] = meta
            if not part:
                outs[3 + k][:, :size] = tok[:, start : start + size]
                outs[3 + k][:, size:] = meta


def prepare(tokens, info, tokens2, info2, starts, sizes):
    rows = tokens.shape[0]
    return pl.pallas_call(
        functools.partial(prep_kernel, starts, sizes),
        out_shape=[jax.ShapeDtypeStruct((2 * rows, size + META), BF16) for size in sizes]
        + [jax.ShapeDtypeStruct((rows, size + META), BF16) for size in sizes],
        compiler_params=PARAMS,
        cost_estimate=cost(0, 10 * tokens.size),
        name="prep",
    )(tokens, info, tokens2, info2)


def slot_matrices(metas, experts, weighted):
    shape = metas[0].shape
    row, lane = iota(shape, 0), iota(shape, 1)
    near = (shape[0], shape[0])
    before = (iota(near, 0) // 8 == iota(near, 1) // 8) & (iota(near, 1) < iota(near, 0))
    before = jnp.where(before, 1.0, 0.0).astype(BF16)
    fits = row // 8 == lane % 16 // 2
    slot = (lane % 2).astype(F32)
    targets = [expert.astype(F32) for expert in experts]
    chosen, weight = [], []
    for meta in metas:
        meta = meta.astype(F32)
        gains = pltpu.roll(meta, META - 8, 1) + pltpu.roll(meta, META - 16, 1) if weighted else None
        picked, gained = jnp.zeros(shape, F32), jnp.zeros(shape, F32)
        for o3 in range(RING):
            hit = (meta == targets[o3]) & (lane < 8)
            here = lane // 16 == o3
            match = jnp.max(jnp.where(hit, 1.0, 0.0), axis=1, keepdims=True)
            picked = jnp.where(here, match, picked)
            if weighted:
                gain = jnp.sum(jnp.where(hit, gains, 0.0), axis=1, keepdims=True)
                gained = jnp.where(here, gain, gained)
        chosen.append(picked)
        weight.append(gained)
    ranks = jnp.dot(
        before,
        jnp.concatenate([picked.astype(BF16) for picked in chosen], axis=1),
        preferred_element_type=F32,
    )
    out = []
    for j, picked in enumerate(chosen):
        keep = (ranks[:, META * j : META * j + META] == slot) & fits
        out.append(jnp.where(keep, picked * weight[j] if weighted else picked, 0.0))
    return out


def split_blocks(refs, size=None):
    return [ref.at[pl.ds(at, 64)] for ref in refs for at in range(0, ref.shape[0], 64)]


def pack_kernel(size, color, experts_ref, *refs):
    blocks, outs = split_blocks(refs[:6]), refs[6:]
    experts = [experts_ref[color, group] for group in range(4)]
    matrices = slot_matrices([block[:, size:] for block in blocks], experts, False)
    matrices = [matrix.T.astype(BF16)[:64] for matrix in matrices]
    for j, block in enumerate(blocks):
        packed = jnp.dot(matrices[j], block[:, :size], preferred_element_type=F32).astype(BF16)
        at = slice(16 * j, 16 * j + 16)
        outs[0][at, :] = packed[:16]
        outs[1][at, :] = packed[16:32]
        outs[1][128 + 16 * j : 128 + 16 * j + 16, :] = packed[32:48]
        outs[2][at, :] = packed[48:]


def pack(blocks, experts, color, size):
    return pl.pallas_call(
        functools.partial(pack_kernel, size, color),
        out_shape=[jax.ShapeDtypeStruct((rows, size), BF16) for rows in (128, 256, 128)],
        in_specs=[pl.BlockSpec(memory_space=pltpu.SMEM)]
        + [pl.BlockSpec(memory_space=pltpu.VMEM)] * 6,
        compiler_params=PARAMS,
        cost_estimate=cost(2 * 64 * 512 * size, 2 * 1024 * size),
        name=f"pack{color}",
    )(experts, *blocks)


def gains_kernel(color, experts_ref, *refs):
    metas, out = split_blocks(refs[:6]), refs[6]
    experts = [experts_ref[color, group] for group in range(4)]
    for j, matrix in enumerate(slot_matrices([meta[...] for meta in metas], experts, True)):
        high = matrix.astype(BF16).astype(F32)
        both = jnp.where(iota(matrix.shape, 1) < 64, high, pltpu.roll(matrix - high, 64, 1))
        out[64 * j : 64 * j + 64, :] = both.astype(BF16)


def gain_matrices(blocks, experts, color, size):
    return pl.pallas_call(
        functools.partial(gains_kernel, color),
        grid=(1,),
        out_shape=jax.ShapeDtypeStruct((512, META), BF16),
        in_specs=[pl.BlockSpec(memory_space=pltpu.SMEM)]
        + [pl.BlockSpec((block.shape[0], META), lambda i: (0, size // META)) for block in blocks],
        out_specs=pl.BlockSpec((512, META), lambda i: (0, 0)),
        compiler_params=PARAMS,
        cost_estimate=cost(0, 512 * 512),
        name=f"gains{color}",
    )(experts, *blocks)


def turned(units):
    return [dict({a: -u[a] % RING for a in "xyz"}, c=u["c"] ^ 1) for u in units]


def moved(units, axis, offset):
    return [dict(u, **{axis: (u[axis] + offset) % RING}) for u in units]


def chunk_places(color):
    a1, a2, a3 = ORDERS[color]
    mine = [{"x": 0, "y": 0, "z": 0, "c": 0}]
    for axis in (a1, a2):
        mine = mine + moved(mine + turned(mine), axis, -1) + moved(mine, axis, 2)
    chip = mine + turned(mine)
    near = moved(chip, a3, -1)
    units = chip + near + turned(near) + moved(chip, a3, 2)
    return [(u["x"], u["y"], u["z"], u["c"]) for u in units]


def chunk_order(color):
    mine = {place: j for j, place in enumerate(chunk_places(color))}
    return [mine[place] for place in chunk_places(0)]


def project_kernel(color, start, size, last, *refs):
    refs = list(refs)
    rows = [refs.pop(0) for _ in range(RING)]
    gate_ref, up_ref = refs.pop(0), refs.pop(0)
    before = refs.pop(0) if color else None
    outs = [refs.pop(0) for _ in range(3 if last else 1)]
    held, gate, up, part, sems = refs
    width = gate.shape[1]
    loads = [
        pltpu.make_async_copy(
            rows[o3].at[pl.ds(0, 128)], held.at[pl.ds(128 * o3, 128)], sems.at[o3]
        )
        for o3 in range(RING)
    ]
    loads.append(pltpu.make_async_copy(gate_ref.at[pl.ds(start, size)], gate, sems.at[4]))
    loads.append(pltpu.make_async_copy(up_ref.at[pl.ds(start, size)], up, sems.at[5]))
    for load in loads:
        load.start()
    for load in loads[:5]:
        load.wait()
    acc = part if color else outs[0]
    for half, weight in enumerate((gate, up)):
        if half:
            loads[5].wait()

        @pl.loop(0, width // 256)
        def _(n, weight=weight, half=half):
            at = pl.multiple_of(n * 256, 256)
            to = pl.multiple_of(half * width + n * 256, 256)
            acc[:, pl.ds(to, 256)] = jnp.dot(
                held[...], weight[:, pl.ds(at, 256)], preferred_element_type=F32
            )

    if not color:
        return
    order = chunk_order(color)
    for i in range(0, 128, 2):
        mine = jnp.concatenate([part[4 * j : 4 * j + 4, :] for j in order[i : i + 2]], axis=0)
        total = before[4 * i : 4 * i + 8, :] + mine
        if not last:
            outs[0][4 * i : 4 * i + 8, :] = total
        else:
            gated, upped = total[:, :width], total[:, width:]
            before[4 * i : 4 * i + 8, :width] = gated / (1.0 + jnp.exp(-gated)) * upped
    if last:
        for k, out in enumerate(outs):
            to_own = chunk_order(k)
            from_own = [to_own.index(j) for j in range(128)]
            for j in range(0, 128, 4):
                out[4 * j : 4 * j + 16, :] = jnp.concatenate(
                    [before[4 * i : 4 * i + 4, :width] for i in from_own[j : j + 4]], axis=0
                ).astype(BF16)


def project(rows, gate, up, before, color, start, size, last):
    width = gate.shape[1]
    everywhere = pl.BlockSpec(memory_space=pl.ANY)
    in_vmem = pl.BlockSpec(memory_space=pltpu.VMEM)
    operands = [*rows, gate, up]
    if color:
        operands.append(before)
    if last:
        outs = [jax.ShapeDtypeStruct((512, width), BF16)] * 3
    else:
        outs = [jax.ShapeDtypeStruct((512, 2 * width), F32)]
    return pl.pallas_call(
        functools.partial(project_kernel, color, start, size, last),
        out_shape=outs,
        in_specs=[everywhere] * 6 + [in_vmem] * (len(operands) - 6),
        scratch_shapes=[
            pltpu.VMEM((512, size), BF16),
            pltpu.VMEM((size, width), BF16),
            pltpu.VMEM((size, width), BF16),
            pltpu.VMEM((512, 2 * width) if color else (8, 128), F32),
            pltpu.SemaphoreType.DMA((6,)),
        ],
        compiler_params=PARAMS,
        cost_estimate=cost(4 * 512 * size * width, 4 * size * width + 2 * 512 * size),
        name=f"project{color}",
    )(*operands)


def down_kernel(start, size, hidden_ref, down_ref, *refs):
    outs, held, sems = refs[:RING], refs[RING], refs[RING + 1]
    step = 512
    loads = []
    for n in range(0, size, step):
        wide = min(step, size - n)
        loads.append(
            pltpu.make_async_copy(
                down_ref.at[:, pl.ds(start + n, wide)],
                held.at[:, pl.ds(n, wide)],
                sems.at[n // step],
            )
        )
        loads[-1].start()
    for n in range(0, size, step):
        loads[n // step].wait()
        to = min(n + step, size)
        value = jnp.dot(hidden_ref[...], held[:, n:to], preferred_element_type=F32).astype(BF16)
        for o3 in range(RING):
            outs[o3][:, n:to] = value[128 * o3 : 128 * o3 + 128]


def project_down(hidden, down, color, start, size):
    return pl.pallas_call(
        functools.partial(down_kernel, start, size),
        out_shape=[jax.ShapeDtypeStruct((128, size), BF16)] * RING,
        in_specs=[pl.BlockSpec(memory_space=pltpu.VMEM), pl.BlockSpec(memory_space=pl.ANY)],
        scratch_shapes=[pltpu.VMEM((down.shape[0], size), BF16), pltpu.SemaphoreType.DMA((5,))],
        compiler_params=PARAMS,
        cost_estimate=cost(2 * 512 * size * 512, 4 * 512 * size),
        name=f"down{color}",
    )(hidden, down)


def weighted_block(gains_ref, back, j):
    at = slice(16 * j, 16 * j + 16)
    rows = [back[0][at, :], back[1][at, :], back[1][128 + 16 * j : 144 + 16 * j, :], back[2][at, :]]
    return jnp.dot(
        gains_ref[64 * j : 64 * j + 64, :],
        jnp.concatenate(rows + rows, axis=0),
        preferred_element_type=F32,
    )


def other_kernel(gains_ref, *refs):
    back, out = refs[:3], refs[3]
    for j in range(4):
        out[64 * j : 64 * j + 64, :] = weighted_block(gains_ref, back, 4 + j).astype(BF16)


def own_kernel(gains_ref, *refs):
    back, swapped, outs = refs[:3], refs[3], refs[4:]
    total = [
        weighted_block(gains_ref, back, j) + swapped[64 * j : 64 * j + 64, :].astype(F32)
        for j in range(4)
    ]
    outs[0][...] = total[0]
    outs[1][:64, :] = total[1].astype(BF16)
    outs[1][64:, :] = total[2].astype(BF16)
    outs[2][...] = total[3].astype(BF16)


def combine(gains, back, swapped, color, size):
    own = swapped is not None
    operands = [gains, *back, swapped] if own else [gains, *back]
    shapes = [(64, F32), (128, BF16), (64, BF16)] if own else [(256, BF16)]
    return pl.pallas_call(
        own_kernel if own else other_kernel,
        out_shape=[jax.ShapeDtypeStruct((rows, size), kind) for rows, kind in shapes],
        compiler_params=PARAMS,
        cost_estimate=cost(4 * 256 * 64 * size, 2 * 512 * size),
        name=f"{'own' if own else 'other'}{color}",
    )(*operands)


def sum_kernel(mine_ref, near_ref, far_ref, cross_ref, *outs):
    total = mine_ref[...] + near_ref[:64, :].astype(F32)
    total = total + far_ref[...].astype(F32) + cross_ref[...].astype(F32)
    outs[0][...] = total[:16]
    outs[1][...] = total[16:48].astype(BF16)
    outs[2][...] = total[48:].astype(BF16)


def sum_blocks(mine, near, far, cross, color, size):
    return pl.pallas_call(
        sum_kernel,
        out_shape=[
            jax.ShapeDtypeStruct((16, size), F32),
            jax.ShapeDtypeStruct((32, size), BF16),
            jax.ShapeDtypeStruct((16, size), BF16),
        ],
        compiler_params=PARAMS,
        cost_estimate=cost(256 * size, 1024 * size),
        name=f"sum{color}",
    )(mine, near, far, cross)


def cross_kernel(starts, sizes, *refs):
    out = refs[-1]
    for ref, start, size in zip(refs, starts, sizes, strict=False):
        out[:, start : start + size] = ref[16:, :]


def cross_rows(near, starts, sizes, rows, width):
    return pl.pallas_call(
        functools.partial(cross_kernel, starts, sizes),
        out_shape=jax.ShapeDtypeStruct((rows, width), BF16),
        compiler_params=PARAMS,
        cost_estimate=cost(0, 4 * rows * width),
        name="cross",
    )(*near)


def finish_kernel(starts, sizes, crossed_ref, *refs):
    out = refs[-1]
    for k, (start, size) in enumerate(zip(starts, sizes, strict=True)):
        mine, near, far = refs[3 * k : 3 * k + 3]
        at = slice(start, start + size)
        total = mine[...] + near[:16, :].astype(F32) + far[...].astype(F32)
        out[:, at] = (total + crossed_ref[:, at].astype(F32)).astype(BF16)


def finish(crossed, pieces, starts, sizes, rows, width):
    return pl.pallas_call(
        functools.partial(finish_kernel, starts, sizes),
        out_shape=jax.ShapeDtypeStruct((rows, width), BF16),
        compiler_params=PARAMS,
        cost_estimate=cost(4 * rows * width, 10 * rows * width),
        name="finish",
    )(crossed, *pieces)


COLORS = range(3)


def body(tokens, routes, route_weight, gate_weight, up_weight, down_weight):
    micro, count, width = tokens.shape
    rows = micro * count
    choices = routes.shape[2]
    starts, sizes = column_split(width)
    node, local = lax.axis_index("node"), lax.axis_index("local")
    here = {"z": node // 2, "c": node % 2, "x": local // 4, "y": local % 4}
    sign = 1 - 2 * here["c"]

    def expert_at(axis, offset, core):
        place = dict(here)
        place[axis] = (here[axis] + sign * offset) % RING
        place["c"] = (here["c"] + core) % 2
        return (place["z"] * 2 + place["c"]) * 8 + (place["x"] * 4 + place["y"]) // 2

    groups = ((0, 0), (1, 0), (1, 1), (2, 0))
    experts = jnp.stack(
        [jnp.stack([expert_at(order[2], *group) for group in groups]) for order in ORDERS]
    ).astype(jnp.int32)
    gains = route_weight.reshape(rows, choices)
    info = jnp.concatenate(
        [
            routes.reshape(rows, choices).astype(F32),
            gains,
            gains,
            jnp.zeros((rows, META - 3 * choices), F32),
        ],
        axis=1,
    )
    flat = tokens.reshape(rows, width)
    prepared = prepare(
        flat, info, from_offset(flat, "c", 1), from_offset(info, "c", 1), starts, sizes
    )
    chip, mine = prepared[:3], prepared[3:]

    near = [from_offset(chip[k], ORDERS[k][0], -1) for k in COLORS]
    far = [from_offset(mine[k], ORDERS[k][0], 2) for k in COLORS]
    mine = [jnp.concatenate([mine[k], near[k], far[k]], axis=0) for k in COLORS]
    far = [from_offset(mine[k], ORDERS[k][1], 2) for k in COLORS]
    theirs = [from_offset(mine[k], "c", 1) for k in COLORS]
    chip = [jnp.concatenate([mine[k], theirs[k]], axis=0) for k in COLORS]
    near = [from_offset(chip[k], ORDERS[k][1], -1) for k in COLORS]
    their_far = [from_offset(far[k], "c", 1) for k in COLORS]
    their_near = [from_offset(near[k], "c", 1) for k in COLORS]
    blocks = [
        [mine[k], near[k], far[k], theirs[k], their_near[k], their_far[k]] for k in COLORS
    ]
    packed = [pack(blocks[k], experts, k, sizes[k]) for k in COLORS]
    near = [from_offset(packed[k][1], ORDERS[k][2], -1) for k in COLORS]
    far = [from_offset(packed[k][2], ORDERS[k][2], 2) for k in COLORS]
    crossed = [from_offset(near[k][128:], "c", 1) for k in COLORS]
    weights = [gain_matrices(blocks[k], experts, k, sizes[k]) for k in COLORS]
    kept, weights = lax.optimization_barrier(([packed[k][0] for k in COLORS], weights))

    hidden = None
    for k in COLORS:
        landed = [kept[k], near[k], crossed[k], far[k]]
        hidden = project(
            landed, gate_weight[0], up_weight[0], hidden, k, starts[k], sizes[k], k == 2
        )
        if k < 2:
            hidden = hidden[0]

    outs = [project_down(hidden[k], down_weight[0], k, starts[k], sizes[k]) for k in COLORS]
    crossed = [from_offset(outs[k][2], "c", 1) for k in COLORS]
    far = [from_offset(outs[k][3], ORDERS[k][2], 2) for k in COLORS]
    near = [jnp.concatenate([outs[k][1], crossed[k]], axis=0) for k in COLORS]
    near = [from_offset(near[k], ORDERS[k][2], 1) for k in COLORS]
    back = [[outs[k][0], near[k], far[k]] for k in COLORS]
    theirs = [combine(weights[k], back[k], None, k, sizes[k])[0] for k in COLORS]
    swapped = [from_offset(theirs[k], "c", 1) for k in COLORS]
    sums = [combine(weights[k], back[k], swapped[k], k, sizes[k]) for k in COLORS]
    near = [from_offset(sums[k][1], ORDERS[k][1], 1) for k in COLORS]
    far = [from_offset(sums[k][2], ORDERS[k][1], 2) for k in COLORS]
    crossed = [from_offset(near[k][64:], "c", 1) for k in COLORS]
    parts = [sum_blocks(sums[k][0], near[k], far[k], crossed[k], k, sizes[k]) for k in COLORS]
    near = [from_offset(parts[k][1], ORDERS[k][0], 1) for k in COLORS]
    far = [from_offset(parts[k][2], ORDERS[k][0], 2) for k in COLORS]
    crossed = from_offset(cross_rows(near, starts, sizes, rows, width), "c", 1)
    pieces = []
    for k in COLORS:
        pieces += [parts[k][0], near[k], far[k]]
    return finish(crossed, pieces, starts, sizes, rows, width).reshape(micro, count, width)


def solution(mesh):
    placed = (
        P(None, AXES, None),
        P(None, AXES, None),
        P(None, AXES, None),
        P(AXES, None, None),
        P(AXES, None, None),
        P(AXES, None, None),
    )
    return jax.shard_map(
        body,
        mesh=mesh,
        in_specs=placed,
        out_specs=P(None, AXES, None),
        check_vma=False,
    )
```

```python
import functools

import jax
import jax.numpy as jnp
from jax import lax
from jax.experimental import pallas as pl
from jax.experimental.pallas import tpu as pltpu
from jax.sharding import PartitionSpec as P

AXES = ("node", "local")
ORDERS = (("x", "y", "z"), ("y", "z", "x"), ("z", "x", "y"))
RING = 4
META = 128
WIDE_PARAMS = pltpu.CompilerParams(vmem_limit_bytes=52 * 1024 * 1024)
PARAMS = pltpu.CompilerParams(vmem_limit_bytes=24 * 1024 * 1024)
BF16, F32 = jnp.bfloat16, jnp.float32


def device_index(place):
    return (place["z"] * 2 + place["c"]) * 16 + place["x"] * 4 + place["y"]


def all_places():
    return [
        {"z": z, "c": c, "x": x, "y": y}
        for z in range(4)
        for c in range(2)
        for x in range(4)
        for y in range(4)
    ]


def from_offset(value, axis, offset):
    size = 2 if axis == "c" else RING
    pairs = []
    for place in all_places():
        sign = -1 if place["c"] else 1
        target = dict(place)
        target[axis] = (place[axis] - sign * offset) % size
        pairs.append((device_index(place), device_index(target)))
    return lax.ppermute(value, AXES, pairs)


def column_split(width):
    tiles = width // 128
    sizes = [(tiles + 2 - k) // 3 * 128 for k in range(3)]
    starts = [sum(sizes[:k]) for k in range(3)]
    return starts, sizes


def cost(flops, nbytes):
    return pl.CostEstimate(flops=int(flops), bytes_accessed=int(nbytes), transcendentals=0)


def iota(shape, dim):
    return lax.broadcasted_iota(jnp.int32, shape, dim)


def prep_kernel(starts, sizes, tok_ref, info_ref, tok2_ref, info2_ref, *outs):
    half = tok_ref.shape[0]
    for part, (tok, info_in) in enumerate(((tok_ref, info_ref), (tok2_ref, info2_ref))):
        info = info_in[...]
        lane = iota(info.shape, 1)
        high = info.astype(BF16)
        low = (info - high.astype(F32)).astype(BF16)
        meta = jnp.where(lane < 16, high.astype(F32), low.astype(F32)).astype(BF16)
        at = slice(part * half, part * half + half)
        for k, (start, size) in enumerate(zip(starts, sizes, strict=True)):
            outs[k][at, :size] = tok[:, start : start + size]
            outs[k][at, size:] = meta
            if not part:
                outs[3 + k][:, :size] = tok[:, start : start + size]
                outs[3 + k][:, size:] = meta


def prepare(tokens, info, tokens2, info2, starts, sizes):
    rows = tokens.shape[0]
    return pl.pallas_call(
        functools.partial(prep_kernel, starts, sizes),
        out_shape=[jax.ShapeDtypeStruct((2 * rows, size + META), BF16) for size in sizes]
        + [jax.ShapeDtypeStruct((rows, size + META), BF16) for size in sizes],
        compiler_params=PARAMS,
        cost_estimate=cost(0, 10 * tokens.size),
        name="prep",
    )(tokens, info, tokens2, info2)


def slot_matrices(metas, experts):
    shape = metas[0].shape
    row, lane = iota(shape, 0), iota(shape, 1)
    near = (shape[0], shape[0])
    before = (iota(near, 0) // 8 == iota(near, 1) // 8) & (iota(near, 1) < iota(near, 0))
    before = jnp.where(before, 1.0, 0.0).astype(BF16)
    fits = row // 8 == lane % 16 // 2
    slot = (lane % 2).astype(F32)
    targets = [expert.astype(F32) for expert in experts]
    gained = []
    for meta in metas:
        meta = meta.astype(F32)
        gains = 4.0 + pltpu.roll(meta, META - 8, 1) + pltpu.roll(meta, META - 16, 1)
        value = jnp.zeros(shape, F32)
        for group in range(4):
            hit = (meta == targets[group]) & (lane < 8)
            gain = jnp.sum(jnp.where(hit, gains, 0.0), axis=1, keepdims=True)
            value = jnp.where(lane // 16 == group, gain, value)
        gained.append(value)
    chosen = [jnp.where(value > 2.0, 1.0, 0.0) for value in gained]
    ranks = jnp.dot(
        before,
        jnp.concatenate([picked.astype(BF16) for picked in chosen], axis=1),
        preferred_element_type=F32,
    )
    out = []
    for j, picked in enumerate(chosen):
        keep = (ranks[:, META * j : META * j + META] == slot) & fits & (picked > 0.5)
        out.append((jnp.where(keep, 1.0, 0.0), jnp.where(keep, gained[j] - 4.0, 0.0)))
    return out


def split_blocks(refs):
    chip, near, far, their_near, their_far = refs
    places = [(chip, 0), (near, 0), (near, 64), (far, 0)]
    places += [(chip, 64), (their_near, 0), (their_near, 64), (their_far, 0)]
    return [ref.at[pl.ds(at, 64)] for ref, at in places]


def pack_kernel(size, color, experts_ref, *refs):
    blocks, outs, gains = split_blocks(refs[:5]), refs[5:8], refs[8]
    experts = [experts_ref[color, group] for group in range(4)]
    matrices = slot_matrices([block[:, size:] for block in blocks], experts)
    slots = [matrix.T.astype(BF16)[:64] for matrix, _ in matrices]
    for j, block in enumerate(blocks):
        packed = jnp.dot(slots[j], block[:, :size], preferred_element_type=F32).astype(BF16)
        at = slice(16 * j, 16 * j + 16)
        outs[0][at, :] = packed[:16]
        outs[1][at, :] = packed[16:32]
        outs[1][128 + 16 * j : 128 + 16 * j + 16, :] = packed[32:48]
        outs[2][at, :] = packed[48:]
    for j, (_, matrix) in enumerate(matrices):
        high = matrix.astype(BF16).astype(F32)
        both = jnp.where(iota(matrix.shape, 1) < 64, high, pltpu.roll(matrix - high, 64, 1))
        gains[64 * j : 64 * j + 64, :] = both.astype(BF16)


def pack(blocks, experts, color, size):
    return pl.pallas_call(
        functools.partial(pack_kernel, size, color),
        out_shape=[jax.ShapeDtypeStruct((rows, size), BF16) for rows in (128, 256, 128)]
        + [jax.ShapeDtypeStruct((512, META), BF16)],
        in_specs=[pl.BlockSpec(memory_space=pltpu.SMEM)]
        + [pl.BlockSpec(memory_space=pltpu.VMEM)] * 5,
        compiler_params=PARAMS,
        cost_estimate=cost(2 * 64 * 512 * size, 2 * 1024 * size),
        name=f"pack{color}",
    )(experts, *blocks)


def turned(units):
    return [dict({a: -u[a] % RING for a in "xyz"}, c=u["c"] ^ 1) for u in units]


def moved(units, axis, offset):
    return [dict(u, **{axis: (u[axis] + offset) % RING}) for u in units]


def chunk_places(color):
    a1, a2, a3 = ORDERS[color]
    mine = [{"x": 0, "y": 0, "z": 0, "c": 0}]
    for axis in (a1, a2):
        mine = mine + moved(mine + turned(mine), axis, -1) + moved(mine, axis, 2)
    chip = mine + turned(mine)
    near = moved(chip, a3, -1)
    units = chip + near + turned(near) + moved(chip, a3, 2)
    return [(u["x"], u["y"], u["z"], u["c"]) for u in units]


def chunk_order(color):
    mine = {place: j for j, place in enumerate(chunk_places(color))}
    return [mine[place] for place in chunk_places(0)]


STEP = 512


def expert_kernel(starts, sizes, *refs):
    refs = list(refs)
    rows = [[refs.pop(0) for _ in range(4)] for _ in sizes]
    gate_ref, up_ref, down_ref = (refs.pop(0) for _ in range(3))
    outs = [[refs.pop(0) for _ in range(4)] for _ in sizes]
    held = [refs.pop(0) for _ in sizes]
    gate, up, down, part, acc, hidden, sems, out_sems = refs
    width = gate.shape[1]
    loads = []
    for k, (start, size) in enumerate(zip(starts, sizes, strict=True)):
        mine = [
            pltpu.make_async_copy(
                rows[k][i].at[pl.ds(0, 128)], held[k].at[pl.ds(128 * i, 128)], sems.at[k, i]
            )
            for i in range(4)
        ]
        span = pl.ds(start, size)
        mine.append(pltpu.make_async_copy(gate_ref.at[span], gate.at[span], sems.at[k, 4]))
        mine.append(pltpu.make_async_copy(up_ref.at[span], up.at[span], sems.at[k, 5]))
        loads.append(mine)
    downs = [
        pltpu.make_async_copy(
            down_ref.at[:, pl.ds(start, size)], down.at[:, pl.ds(start, size)], sems.at[k, 6]
        )
        for k, (start, size) in enumerate(zip(starts, sizes, strict=True))
    ]
    for load in [*loads[0], *loads[1], *loads[2], *downs]:
        load.start()
    for k, (start, size) in enumerate(zip(starts, sizes, strict=True)):
        for load in loads[k][:5]:
            load.wait()
        into = part if k else acc
        for half, weight in enumerate((gate, up)):
            if half:
                loads[k][5].wait()

            @pl.loop(0, width // 256)
            def _(n, weight=weight, half=half, into=into, k=k, start=start, size=size):
                at = pl.multiple_of(n * 256, 256)
                to = pl.multiple_of(half * width + n * 256, 256)
                into[:, pl.ds(to, 256)] = jnp.dot(
                    held[k][...],
                    weight[start : start + size, pl.ds(at, 256)],
                    preferred_element_type=F32,
                )

        if not k:
            continue
        order = chunk_order(k)
        for i in range(0, 128, 2):
            mine = jnp.concatenate([part[4 * j : 4 * j + 4, :] for j in order[i : i + 2]], axis=0)
            total = acc[4 * i : 4 * i + 8, :] + mine
            if k < 2:
                acc[4 * i : 4 * i + 8, :] = total
            else:
                gated, upped = total[:, :width], total[:, width:]
                acc[4 * i : 4 * i + 8, :width] = gated / (1.0 + jnp.exp(-gated)) * upped
    sends = []
    for k, (start, size) in enumerate(zip(starts, sizes, strict=True)):
        to_own = chunk_order(k)
        from_own = [to_own.index(j) for j in range(128)]
        for j in range(0, 128, 4):
            hidden[4 * j : 4 * j + 16, :] = jnp.concatenate(
                [acc[4 * i : 4 * i + 4, :width] for i in from_own[j : j + 4]], axis=0
            ).astype(BF16)
        downs[k].wait()
        for n in range(0, size, STEP):
            to = min(n + STEP, size)
            held[k][:, n:to] = jnp.dot(
                hidden[...], down[:, start + n : start + to], preferred_element_type=F32
            ).astype(BF16)
        for i in range(4):
            sends.append(
                pltpu.make_async_copy(
                    held[k].at[pl.ds(128 * i, 128)], outs[k][i], out_sems.at[k, i]
                )
            )
            sends[-1].start()
    for send in sends:
        send.wait()


def expert_halves(rows, gate, up, down, starts, sizes):
    width = gate.shape[1]
    everywhere = pl.BlockSpec(memory_space=pl.ANY)
    results = pl.pallas_call(
        functools.partial(expert_kernel, starts, sizes),
        out_shape=[jax.ShapeDtypeStruct((128, size), BF16) for size in sizes for _ in range(4)],
        in_specs=[everywhere] * 15,
        out_specs=[everywhere] * 12,
        scratch_shapes=[pltpu.VMEM((512, size), BF16) for size in sizes]
        + [
            pltpu.VMEM(gate.shape, BF16),
            pltpu.VMEM(up.shape, BF16),
            pltpu.VMEM(down.shape, BF16),
            pltpu.VMEM((512, 2 * width), F32),
            pltpu.VMEM((512, 2 * width), F32),
            pltpu.VMEM((512, width), BF16),
            pltpu.SemaphoreType.DMA((3, 7)),
            pltpu.SemaphoreType.DMA((3, 4)),
        ],
        compiler_params=WIDE_PARAMS,
        cost_estimate=cost(6 * 512 * gate.size, 6 * gate.size + 4 * 512 * gate.shape[0]),
        name="experts",
    )(*[ref for mine in rows for ref in mine], gate, up, down)
    return [results[4 * k : 4 * k + 4] for k in range(3)]


def weighted_block(gains_ref, back, j):
    at = slice(16 * j, 16 * j + 16)
    rows = [back[0][at, :], back[1][at, :], back[1][128 + 16 * j : 144 + 16 * j, :], back[2][at, :]]
    return jnp.dot(
        gains_ref[64 * j : 64 * j + 64, :],
        jnp.concatenate(rows + rows, axis=0),
        preferred_element_type=F32,
    )


def other_kernel(gains_ref, *refs):
    back, out = refs[:3], refs[3]
    for j in range(4):
        out[64 * j : 64 * j + 64, :] = weighted_block(gains_ref, back, 4 + j).astype(BF16)


def own_kernel(gains_ref, *refs):
    back, swapped, outs = refs[:3], refs[3], refs[4:]
    total = [
        weighted_block(gains_ref, back, j) + swapped[64 * j : 64 * j + 64, :].astype(F32)
        for j in range(4)
    ]
    outs[0][...] = total[0]
    outs[1][:64, :] = total[1].astype(BF16)
    outs[1][64:, :] = total[2].astype(BF16)
    outs[2][...] = total[3].astype(BF16)


def combine(gains, back, swapped, color, size):
    own = swapped is not None
    operands = [gains, *back, swapped] if own else [gains, *back]
    shapes = [(64, F32), (128, BF16), (64, BF16)] if own else [(256, BF16)]
    return pl.pallas_call(
        own_kernel if own else other_kernel,
        out_shape=[jax.ShapeDtypeStruct((rows, size), kind) for rows, kind in shapes],
        compiler_params=PARAMS,
        cost_estimate=cost(4 * 256 * 64 * size, 2 * 512 * size),
        name=f"{'own' if own else 'other'}{color}",
    )(*operands)


def sum_kernel(mine_ref, near_ref, far_ref, cross_ref, *outs):
    total = mine_ref[...] + near_ref[:64, :].astype(F32)
    total = total + far_ref[...].astype(F32) + cross_ref[...].astype(F32)
    outs[0][...] = total[:16]
    outs[1][...] = total[16:48].astype(BF16)
    outs[2][...] = total[48:].astype(BF16)


def sum_blocks(mine, near, far, cross, color, size):
    return pl.pallas_call(
        sum_kernel,
        out_shape=[
            jax.ShapeDtypeStruct((16, size), F32),
            jax.ShapeDtypeStruct((32, size), BF16),
            jax.ShapeDtypeStruct((16, size), BF16),
        ],
        compiler_params=PARAMS,
        cost_estimate=cost(256 * size, 1024 * size),
        name=f"sum{color}",
    )(mine, near, far, cross)


def cross_kernel(starts, sizes, *refs):
    out = refs[-1]
    for ref, start, size in zip(refs, starts, sizes, strict=False):
        out[:, start : start + size] = ref[16:, :]


def cross_rows(near, starts, sizes, rows, width):
    return pl.pallas_call(
        functools.partial(cross_kernel, starts, sizes),
        out_shape=jax.ShapeDtypeStruct((rows, width), BF16),
        compiler_params=PARAMS,
        cost_estimate=cost(0, 4 * rows * width),
        name="cross",
    )(*near)


def finish_kernel(starts, sizes, crossed_ref, *refs):
    out = refs[-1]
    for k, (start, size) in enumerate(zip(starts, sizes, strict=True)):
        mine, near, far = refs[3 * k : 3 * k + 3]
        at = slice(start, start + size)
        total = mine[...] + near[:16, :].astype(F32) + far[...].astype(F32)
        out[:, at] = (total + crossed_ref[:, at].astype(F32)).astype(BF16)


def finish(crossed, pieces, starts, sizes, rows, width):
    return pl.pallas_call(
        functools.partial(finish_kernel, starts, sizes),
        out_shape=jax.ShapeDtypeStruct((rows, width), BF16),
        compiler_params=PARAMS,
        cost_estimate=cost(4 * rows * width, 10 * rows * width),
        name="finish",
    )(crossed, *pieces)


COLORS = range(3)


def after(value, earlier):
    return lax.optimization_barrier((value, earlier))


def body(tokens, routes, route_weight, gate_weight, up_weight, down_weight):
    micro, count, width = tokens.shape
    rows = micro * count
    choices = routes.shape[2]
    starts, sizes = column_split(width)
    node, local = lax.axis_index("node"), lax.axis_index("local")
    here = {"z": node // 2, "c": node % 2, "x": local // 4, "y": local % 4}
    sign = 1 - 2 * here["c"]

    def expert_at(axis, offset, core):
        place = dict(here)
        place[axis] = (here[axis] + sign * offset) % RING
        place["c"] = (here["c"] + core) % 2
        return (place["z"] * 2 + place["c"]) * 8 + (place["x"] * 4 + place["y"]) // 2

    groups = ((0, 0), (1, 0), (1, 1), (2, 0))
    experts = jnp.stack(
        [jnp.stack([expert_at(order[2], *group) for group in groups]) for order in ORDERS]
    ).astype(jnp.int32)
    gains = route_weight.reshape(rows, choices)
    info = jnp.concatenate(
        [
            routes.reshape(rows, choices).astype(F32),
            gains,
            gains,
            jnp.zeros((rows, META - 3 * choices), F32),
        ],
        axis=1,
    )
    flat = tokens.reshape(rows, width)
    prepared = prepare(
        flat, info, from_offset(flat, "c", 1), from_offset(info, "c", 1), starts, sizes
    )
    chip, mine = prepared[:3], prepared[3:]

    near = [from_offset(chip[k], ORDERS[k][0], -1) for k in COLORS]
    far = [from_offset(mine[k], ORDERS[k][0], 2) for k in COLORS]
    near, far = after(near, far)
    mine = [jnp.concatenate([mine[k], near[k], far[k]], axis=0) for k in COLORS]
    far = [from_offset(mine[k], ORDERS[k][1], 2) for k in COLORS]
    theirs = [from_offset(mine[k], "c", 1) for k in COLORS]
    chip = [jnp.concatenate([mine[k], theirs[k]], axis=0) for k in COLORS]
    chip, far = after(chip, far)
    near = [from_offset(chip[k], ORDERS[k][1], -1) for k in COLORS]
    their_far = [from_offset(far[k], "c", 1) for k in COLORS]
    near, their_far = after(near, their_far)
    their_near = [from_offset(near[k], "c", 1) for k in COLORS]
    blocks = [[chip[k], near[k], far[k], their_near[k], their_far[k]] for k in COLORS]
    packed = [pack(blocks[k], experts, k, sizes[k]) for k in COLORS]
    near = [from_offset(packed[k][1], ORDERS[k][2], -1) for k in COLORS]
    far = [packed[k][2] for k in COLORS]
    for k in COLORS:
        far[k], near[k] = after(far[k], near[k])
    far = [from_offset(far[k], ORDERS[k][2], 2) for k in COLORS]
    crossed = [from_offset(near[k][128:], "c", 1) for k in COLORS]

    landed = [[packed[k][0], near[k], crossed[k], far[k]] for k in COLORS]
    outs = expert_halves(
        landed, gate_weight[0], up_weight[0], down_weight[0], starts, sizes
    )

    crossed = [from_offset(outs[k][2], "c", 1) for k in COLORS]
    far = [from_offset(outs[k][3], ORDERS[k][2], 2) for k in COLORS]
    near = [jnp.concatenate([outs[k][1], crossed[k]], axis=0) for k in COLORS]
    near = [from_offset(near[k], ORDERS[k][2], 1) for k in COLORS]
    back = [[outs[k][0], near[k], far[k]] for k in COLORS]
    theirs = [combine(packed[k][3], back[k], None, k, sizes[k])[0] for k in COLORS]
    swapped = [from_offset(theirs[k], "c", 1) for k in COLORS]
    sums = [combine(packed[k][3], back[k], swapped[k], k, sizes[k]) for k in COLORS]
    near = [from_offset(sums[k][1], ORDERS[k][1], 1) for k in COLORS]
    far = [sums[k][2] for k in COLORS]
    for k in COLORS:
        far[k], near[k] = after(far[k], near[k])
    far = [from_offset(far[k], ORDERS[k][1], 2) for k in COLORS]
    crossed = [from_offset(near[k][64:], "c", 1) for k in COLORS]
    parts = [sum_blocks(sums[k][0], near[k], far[k], crossed[k], k, sizes[k]) for k in COLORS]
    near = [from_offset(parts[k][1], ORDERS[k][0], 1) for k in COLORS]
    far = [from_offset(parts[k][2], ORDERS[k][0], 2) for k in COLORS]
    crossed = from_offset(cross_rows(near, starts, sizes, rows, width), "c", 1)
    pieces = []
    for k in COLORS:
        pieces += [parts[k][0], near[k], far[k]]
    return finish(crossed, pieces, starts, sizes, rows, width).reshape(micro, count, width)


def solution(mesh):
    placed = (
        P(None, AXES, None),
        P(None, AXES, None),
        P(None, AXES, None),
        P(AXES, None, None),
        P(AXES, None, None),
        P(AXES, None, None),
    )
    return jax.shard_map(
        body,
        mesh=mesh,
        in_specs=placed,
        out_specs=P(None, AXES, None),
        check_vma=False,
    )
```

```python
import functools

import jax
import jax.numpy as jnp
from jax import lax
from jax.experimental import pallas as pl
from jax.experimental.pallas import tpu as pltpu
from jax.sharding import PartitionSpec as P

AXES = ("node", "local")
ORDERS = (("x", "y", "z"), ("y", "z", "x"), ("z", "x", "y"))
RING = 4
META = 128
WIDE_PARAMS = pltpu.CompilerParams(vmem_limit_bytes=40 * 1024 * 1024)
PARAMS = pltpu.CompilerParams(vmem_limit_bytes=14 * 1024 * 1024)
BF16, F32 = jnp.bfloat16, jnp.float32


def device_index(place):
    return (place["z"] * 2 + place["c"]) * 16 + place["x"] * 4 + place["y"]


def all_places():
    return [
        {"z": z, "c": c, "x": x, "y": y}
        for z in range(4)
        for c in range(2)
        for x in range(4)
        for y in range(4)
    ]


def from_offset(value, axis, offset):
    size = 2 if axis == "c" else RING
    pairs = []
    for place in all_places():
        sign = -1 if place["c"] else 1
        target = dict(place)
        target[axis] = (place[axis] - sign * offset) % size
        pairs.append((device_index(place), device_index(target)))
    return lax.ppermute(value, AXES, pairs)


def column_split(width):
    tiles = width // 128
    sizes = [(tiles + 2 - k) // 3 * 128 for k in range(3)]
    starts = [sum(sizes[:k]) for k in range(3)]
    return starts, sizes


def cost(flops, nbytes):
    return pl.CostEstimate(flops=int(flops), bytes_accessed=int(nbytes), transcendentals=0)


def iota(shape, dim):
    return lax.broadcasted_iota(jnp.int32, shape, dim)


def prep_kernel(starts, sizes, tok_ref, info_ref, tok2_ref, info2_ref, *outs):
    half = tok_ref.shape[0]
    for part, (tok, info_in) in enumerate(((tok_ref, info_ref), (tok2_ref, info2_ref))):
        info = info_in[...]
        lane = iota(info.shape, 1)
        high = info.astype(BF16)
        low = (info - high.astype(F32)).astype(BF16)
        meta = jnp.where(lane < 16, high.astype(F32), low.astype(F32)).astype(BF16)
        at = slice(part * half, part * half + half)
        for k, (start, size) in enumerate(zip(starts, sizes, strict=True)):
            outs[k][at, :size] = tok[:, start : start + size]
            outs[k][at, size:] = meta
            if not part:
                outs[3 + k][:, :size] = tok[:, start : start + size]
                outs[3 + k][:, size:] = meta


def prepare(tokens, info, tokens2, info2, starts, sizes):
    rows = tokens.shape[0]
    return pl.pallas_call(
        functools.partial(prep_kernel, starts, sizes),
        out_shape=[jax.ShapeDtypeStruct((2 * rows, size + META), BF16) for size in sizes]
        + [jax.ShapeDtypeStruct((rows, size + META), BF16) for size in sizes],
        compiler_params=PARAMS,
        cost_estimate=cost(0, 10 * tokens.size),
        name="prep",
    )(tokens, info, tokens2, info2)


def slot_matrices(metas, experts):
    shape = metas[0].shape
    row, lane = iota(shape, 0), iota(shape, 1)
    near = (shape[0], shape[0])
    before = (iota(near, 0) // 8 == iota(near, 1) // 8) & (iota(near, 1) < iota(near, 0))
    before = jnp.where(before, 1.0, 0.0).astype(BF16)
    fits = row // 8 == lane % 16 // 2
    slot = (lane % 2).astype(F32)
    targets = [expert.astype(F32) for expert in experts]
    gained = []
    for meta in metas:
        meta = meta.astype(F32)
        gains = 4.0 + pltpu.roll(meta, META - 8, 1) + pltpu.roll(meta, META - 16, 1)
        value = jnp.zeros(shape, F32)
        for group in range(4):
            hit = (meta == targets[group]) & (lane < 8)
            gain = jnp.sum(jnp.where(hit, gains, 0.0), axis=1, keepdims=True)
            value = jnp.where(lane // 16 == group, gain, value)
        gained.append(value)
    chosen = [jnp.where(value > 2.0, 1.0, 0.0) for value in gained]
    ranks = jnp.dot(
        before,
        jnp.concatenate([picked.astype(BF16) for picked in chosen], axis=1),
        preferred_element_type=F32,
    )
    out = []
    for j, picked in enumerate(chosen):
        keep = (ranks[:, META * j : META * j + META] == slot) & fits & (picked > 0.5)
        out.append((jnp.where(keep, 1.0, 0.0), jnp.where(keep, gained[j] - 4.0, 0.0)))
    return out


def split_blocks(refs):
    chip, near, far, their_near, their_far = refs
    places = [(chip, 0), (near, 0), (near, 64), (far, 0)]
    places += [(chip, 64), (their_near, 0), (their_near, 64), (their_far, 0)]
    return [ref.at[pl.ds(at, 64)] for ref, at in places]


def pack_kernel(size, color, experts_ref, *refs):
    blocks, outs, gains = split_blocks(refs[:5]), refs[5:8], refs[8]
    experts = [experts_ref[color, group] for group in range(4)]
    matrices = slot_matrices([block[:, size:] for block in blocks], experts)
    slots = [matrix.T.astype(BF16)[:64] for matrix, _ in matrices]
    for j, block in enumerate(blocks):
        packed = jnp.dot(slots[j], block[:, :size], preferred_element_type=F32).astype(BF16)
        at = slice(16 * j, 16 * j + 16)
        outs[0][at, :] = packed[:16]
        outs[1][at, :] = packed[16:32]
        outs[1][128 + 16 * j : 128 + 16 * j + 16, :] = packed[32:48]
        outs[2][at, :] = packed[48:]
    for j, (_, matrix) in enumerate(matrices):
        high = matrix.astype(BF16).astype(F32)
        both = jnp.where(iota(matrix.shape, 1) < 64, high, pltpu.roll(matrix - high, 64, 1))
        gains[64 * j : 64 * j + 64, :] = both.astype(BF16)


def pack(blocks, experts, color, size):
    return pl.pallas_call(
        functools.partial(pack_kernel, size, color),
        out_shape=[jax.ShapeDtypeStruct((rows, size), BF16) for rows in (128, 256, 128)]
        + [jax.ShapeDtypeStruct((512, META), BF16)],
        in_specs=[pl.BlockSpec(memory_space=pltpu.SMEM)]
        + [pl.BlockSpec(memory_space=pltpu.VMEM)] * 5,
        compiler_params=PARAMS,
        cost_estimate=cost(2 * 64 * 512 * size, 2 * 1024 * size),
        name=f"pack{color}",
    )(experts, *blocks)


def turned(units):
    return [dict({a: -u[a] % RING for a in "xyz"}, c=u["c"] ^ 1) for u in units]


def moved(units, axis, offset):
    return [dict(u, **{axis: (u[axis] + offset) % RING}) for u in units]


def chunk_places(color):
    a1, a2, a3 = ORDERS[color]
    mine = [{"x": 0, "y": 0, "z": 0, "c": 0}]
    for axis in (a1, a2):
        mine = mine + moved(mine + turned(mine), axis, -1) + moved(mine, axis, 2)
    chip = mine + turned(mine)
    near = moved(chip, a3, -1)
    units = chip + near + turned(near) + moved(chip, a3, 2)
    return [(u["x"], u["y"], u["z"], u["c"]) for u in units]


def chunk_order(color):
    mine = {place: j for j, place in enumerate(chunk_places(color))}
    return [mine[place] for place in chunk_places(0)]


STEP = 512


def expert_kernel(starts, sizes, *refs):
    refs = list(refs)
    rows = [[refs.pop(0) for _ in range(4)] for _ in sizes]
    gate_ref, up_ref, down_ref = (refs.pop(0) for _ in range(3))
    outs = [[refs.pop(0) for _ in range(4)] for _ in sizes]
    held = [refs.pop(0) for _ in sizes]
    gate, up, down, part, acc, hidden, sems, out_sems = refs
    width = gate.shape[1]
    loads = []
    for k, (start, size) in enumerate(zip(starts, sizes, strict=True)):
        mine = [
            pltpu.make_async_copy(
                rows[k][i].at[pl.ds(0, 128)], held[k].at[pl.ds(128 * i, 128)], sems.at[k, i]
            )
            for i in range(4)
        ]
        span = pl.ds(start, size)
        mine.append(pltpu.make_async_copy(gate_ref.at[span], gate.at[span], sems.at[k, 4]))
        mine.append(pltpu.make_async_copy(up_ref.at[span], up.at[span], sems.at[k, 5]))
        loads.append(mine)
    downs = [
        pltpu.make_async_copy(
            down_ref.at[:, pl.ds(start, size)], down.at[:, pl.ds(start, size)], sems.at[k, 6]
        )
        for k, (start, size) in enumerate(zip(starts, sizes, strict=True))
    ]
    for load in [*loads[0], *loads[1], *loads[2], *downs]:
        load.start()
    for k, (start, size) in enumerate(zip(starts, sizes, strict=True)):
        for load in loads[k][:5]:
            load.wait()
        into = part if k else acc
        for half, weight in enumerate((gate, up)):
            if half:
                loads[k][5].wait()

            @pl.loop(0, width // 256)
            def _(n, weight=weight, half=half, into=into, k=k, start=start, size=size):
                at = pl.multiple_of(n * 256, 256)
                to = pl.multiple_of(half * width + n * 256, 256)
                into[:, pl.ds(to, 256)] = jnp.dot(
                    held[k][...],
                    weight[start : start + size, pl.ds(at, 256)],
                    preferred_element_type=F32,
                )

        if not k:
            continue
        order = chunk_order(k)
        for i in range(0, 128, 2):
            mine = jnp.concatenate([part[4 * j : 4 * j + 4, :] for j in order[i : i + 2]], axis=0)
            total = acc[4 * i : 4 * i + 8, :] + mine
            if k < 2:
                acc[4 * i : 4 * i + 8, :] = total
            else:
                gated, upped = total[:, :width], total[:, width:]
                acc[4 * i : 4 * i + 8, :width] = gated / (1.0 + jnp.exp(-gated)) * upped
    sends = []
    for k, (start, size) in enumerate(zip(starts, sizes, strict=True)):
        to_own = chunk_order(k)
        from_own = [to_own.index(j) for j in range(128)]
        for j in range(0, 128, 4):
            hidden[4 * j : 4 * j + 16, :] = jnp.concatenate(
                [acc[4 * i : 4 * i + 4, :width] for i in from_own[j : j + 4]], axis=0
            ).astype(BF16)
        downs[k].wait()
        for n in range(0, size, STEP):
            to = min(n + STEP, size)
            held[k][:, n:to] = jnp.dot(
                hidden[...], down[:, start + n : start + to], preferred_element_type=F32
            ).astype(BF16)
        for i in range(4):
            sends.append(
                pltpu.make_async_copy(
                    held[k].at[pl.ds(128 * i, 128)], outs[k][i], out_sems.at[k, i]
                )
            )
            sends[-1].start()
    for send in sends:
        send.wait()


def expert_halves(rows, gate, up, down, starts, sizes):
    width = gate.shape[1]
    everywhere = pl.BlockSpec(memory_space=pl.ANY)
    results = pl.pallas_call(
        functools.partial(expert_kernel, starts, sizes),
        out_shape=[jax.ShapeDtypeStruct((128, size), BF16) for size in sizes for _ in range(4)],
        in_specs=[everywhere] * 12 + [pl.BlockSpec(memory_space=pltpu.HBM)] * 3,
        out_specs=[everywhere] * 12,
        scratch_shapes=[pltpu.VMEM((512, size), BF16) for size in sizes]
        + [
            pltpu.VMEM(gate.shape, BF16),
            pltpu.VMEM(up.shape, BF16),
            pltpu.VMEM(down.shape, BF16),
            pltpu.VMEM((512, 2 * width), F32),
            pltpu.VMEM((512, 2 * width), F32),
            pltpu.VMEM((512, width), BF16),
            pltpu.SemaphoreType.DMA((3, 7)),
            pltpu.SemaphoreType.DMA((3, 4)),
        ],
        compiler_params=WIDE_PARAMS,
        cost_estimate=cost(6 * 512 * gate.size, 6 * gate.size + 4 * 512 * gate.shape[0]),
        name="experts",
    )(
        *[ref for mine in rows for ref in mine],
        *[pltpu.with_memory_space_constraint(weight, pltpu.HBM) for weight in (gate, up, down)],
    )
    return [results[4 * k : 4 * k + 4] for k in range(3)]


def weighted_block(gains_ref, back, j):
    at = slice(16 * j, 16 * j + 16)
    rows = [back[0][at, :], back[1][at, :], back[1][128 + 16 * j : 144 + 16 * j, :], back[2][at, :]]
    return jnp.dot(
        gains_ref[64 * j : 64 * j + 64, :],
        jnp.concatenate(rows + rows, axis=0),
        preferred_element_type=F32,
    )


def other_kernel(gains_ref, *refs):
    back, out = refs[:3], refs[3]
    for j in range(4):
        out[64 * j : 64 * j + 64, :] = weighted_block(gains_ref, back, 4 + j).astype(BF16)


def own_kernel(gains_ref, *refs):
    back, swapped, outs = refs[:3], refs[3], refs[4:]
    total = [
        weighted_block(gains_ref, back, j) + swapped[64 * j : 64 * j + 64, :].astype(F32)
        for j in range(4)
    ]
    outs[0][...] = total[0]
    outs[1][:64, :] = total[1].astype(BF16)
    outs[1][64:, :] = total[2].astype(BF16)
    outs[2][...] = total[3].astype(BF16)


def combine(gains, back, swapped, color, size):
    own = swapped is not None
    operands = [gains, *back, swapped] if own else [gains, *back]
    shapes = [(64, F32), (128, BF16), (64, BF16)] if own else [(256, BF16)]
    return pl.pallas_call(
        own_kernel if own else other_kernel,
        out_shape=[jax.ShapeDtypeStruct((rows, size), kind) for rows, kind in shapes],
        compiler_params=PARAMS,
        cost_estimate=cost(4 * 256 * 64 * size, 2 * 512 * size),
        name=f"{'own' if own else 'other'}{color}",
    )(*operands)


def sum_kernel(mine_ref, near_ref, far_ref, cross_ref, *outs):
    total = mine_ref[...] + near_ref[:64, :].astype(F32)
    total = total + far_ref[...].astype(F32) + cross_ref[...].astype(F32)
    outs[0][...] = total[:16]
    outs[1][...] = total[16:48].astype(BF16)
    outs[2][...] = total[48:].astype(BF16)


def sum_blocks(mine, near, far, cross, color, size):
    return pl.pallas_call(
        sum_kernel,
        out_shape=[
            jax.ShapeDtypeStruct((16, size), F32),
            jax.ShapeDtypeStruct((32, size), BF16),
            jax.ShapeDtypeStruct((16, size), BF16),
        ],
        compiler_params=PARAMS,
        cost_estimate=cost(256 * size, 1024 * size),
        name=f"sum{color}",
    )(mine, near, far, cross)


def cross_kernel(starts, sizes, *refs):
    out = refs[-1]
    for ref, start, size in zip(refs, starts, sizes, strict=False):
        out[:, start : start + size] = ref[16:, :]


def cross_rows(near, starts, sizes, rows, width):
    return pl.pallas_call(
        functools.partial(cross_kernel, starts, sizes),
        out_shape=jax.ShapeDtypeStruct((rows, width), BF16),
        compiler_params=PARAMS,
        cost_estimate=cost(0, 4 * rows * width),
        name="cross",
    )(*near)


def finish_kernel(starts, sizes, crossed_ref, *refs):
    out = refs[-1]
    for k, (start, size) in enumerate(zip(starts, sizes, strict=True)):
        mine, near, far = refs[3 * k : 3 * k + 3]
        at = slice(start, start + size)
        total = mine[...] + near[:16, :].astype(F32) + far[...].astype(F32)
        out[:, at] = (total + crossed_ref[:, at].astype(F32)).astype(BF16)


def finish(crossed, pieces, starts, sizes, rows, width):
    return pl.pallas_call(
        functools.partial(finish_kernel, starts, sizes),
        out_shape=jax.ShapeDtypeStruct((rows, width), BF16),
        compiler_params=PARAMS,
        cost_estimate=cost(4 * rows * width, 10 * rows * width),
        name="finish",
    )(crossed, *pieces)


COLORS = range(3)


def after(value, earlier):
    return lax.optimization_barrier((value, earlier))


def body(tokens, routes, route_weight, gate_weight, up_weight, down_weight):
    micro, count, width = tokens.shape
    rows = micro * count
    choices = routes.shape[2]
    starts, sizes = column_split(width)
    node, local = lax.axis_index("node"), lax.axis_index("local")
    here = {"z": node // 2, "c": node % 2, "x": local // 4, "y": local % 4}
    sign = 1 - 2 * here["c"]

    def expert_at(axis, offset, core):
        place = dict(here)
        place[axis] = (here[axis] + sign * offset) % RING
        place["c"] = (here["c"] + core) % 2
        return (place["z"] * 2 + place["c"]) * 8 + (place["x"] * 4 + place["y"]) // 2

    groups = ((0, 0), (1, 0), (1, 1), (2, 0))
    experts = jnp.stack(
        [jnp.stack([expert_at(order[2], *group) for group in groups]) for order in ORDERS]
    ).astype(jnp.int32)
    gains = route_weight.reshape(rows, choices)
    info = jnp.concatenate(
        [
            routes.reshape(rows, choices).astype(F32),
            gains,
            gains,
            jnp.zeros((rows, META - 3 * choices), F32),
        ],
        axis=1,
    )
    flat = tokens.reshape(rows, width)
    prepared = prepare(
        flat, info, from_offset(flat, "c", 1), from_offset(info, "c", 1), starts, sizes
    )
    chip, mine = prepared[:3], prepared[3:]

    near = [from_offset(chip[k], ORDERS[k][0], -1) for k in COLORS]
    far = [from_offset(mine[k], ORDERS[k][0], 2) for k in COLORS]
    near, far = after(near, far)
    mine = [jnp.concatenate([mine[k], near[k], far[k]], axis=0) for k in COLORS]
    far = [from_offset(mine[k], ORDERS[k][1], 2) for k in COLORS]
    theirs = [from_offset(mine[k], "c", 1) for k in COLORS]
    chip = [jnp.concatenate([mine[k], theirs[k]], axis=0) for k in COLORS]
    chip, far = after(chip, far)
    near = [from_offset(chip[k], ORDERS[k][1], -1) for k in COLORS]
    their_far = [from_offset(far[k], "c", 1) for k in COLORS]
    near, their_far = after(near, their_far)
    their_near = [from_offset(near[k], "c", 1) for k in COLORS]
    blocks = [[chip[k], near[k], far[k], their_near[k], their_far[k]] for k in COLORS]
    packed = [pack(blocks[k], experts, k, sizes[k]) for k in COLORS]
    near = [from_offset(packed[k][1], ORDERS[k][2], -1) for k in COLORS]
    far = [packed[k][2] for k in COLORS]
    for k in COLORS:
        far[k], near[k] = after(far[k], near[k])
    far = [from_offset(far[k], ORDERS[k][2], 2) for k in COLORS]
    crossed = [from_offset(near[k][128:], "c", 1) for k in COLORS]

    landed = [[packed[k][0], near[k], crossed[k], far[k]] for k in COLORS]
    outs = expert_halves(
        landed, gate_weight[0], up_weight[0], down_weight[0], starts, sizes
    )

    crossed = [from_offset(outs[k][2], "c", 1) for k in COLORS]
    far = [from_offset(outs[k][3], ORDERS[k][2], 2) for k in COLORS]
    near = [jnp.concatenate([outs[k][1], crossed[k]], axis=0) for k in COLORS]
    near = [from_offset(near[k], ORDERS[k][2], 1) for k in COLORS]
    back = [[outs[k][0], near[k], far[k]] for k in COLORS]
    theirs = [combine(packed[k][3], back[k], None, k, sizes[k])[0] for k in COLORS]
    swapped = [from_offset(theirs[k], "c", 1) for k in COLORS]
    sums = [combine(packed[k][3], back[k], swapped[k], k, sizes[k]) for k in COLORS]
    near = [from_offset(sums[k][1], ORDERS[k][1], 1) for k in COLORS]
    far = [sums[k][2] for k in COLORS]
    for k in COLORS:
        far[k], near[k] = after(far[k], near[k])
    far = [from_offset(far[k], ORDERS[k][1], 2) for k in COLORS]
    crossed = [from_offset(near[k][64:], "c", 1) for k in COLORS]
    parts = [sum_blocks(sums[k][0], near[k], far[k], crossed[k], k, sizes[k]) for k in COLORS]
    near = [from_offset(parts[k][1], ORDERS[k][0], 1) for k in COLORS]
    far = [from_offset(parts[k][2], ORDERS[k][0], 2) for k in COLORS]
    crossed = from_offset(cross_rows(near, starts, sizes, rows, width), "c", 1)
    pieces = []
    for k in COLORS:
        pieces += [parts[k][0], near[k], far[k]]
    return finish(crossed, pieces, starts, sizes, rows, width).reshape(micro, count, width)


def solution(mesh):
    placed = (
        P(None, AXES, None),
        P(None, AXES, None),
        P(None, AXES, None),
        P(AXES, None, None),
        P(AXES, None, None),
        P(AXES, None, None),
    )
    return jax.shard_map(
        body,
        mesh=mesh,
        in_specs=placed,
        out_specs=P(None, AXES, None),
        check_vma=False,
    )
```
